32 devices in a mesh: dp: 4 (over z), ctx: 4 (over y, x), mp: 2 (over core).
Axes of the slice: x: 2, y: 2, z: 4, core: 2. Of those that a mesh axis runs over, the one named last changes fastest.
Arguments:
- llm_grad: bfloat16 [2048, 4096], P(('dp', 'ctx')), may hold values from -6 to 6
- merger_pre: bfloat16 [768, 5120], P(('dp', 'ctx', 'mp')), may hold values from -6 to 6
- out_weight: bfloat16 [5120, 4096], P(('ctx', 'mp')), may hold values from -0.078125 to 0.078125
- patch_counts: int32 [4, 8, 4], P('dp'), may hold values from 1 to 12, 24 in all within a row
- image_order: int32 [4, 32], P('dp'), may hold values from 0 to 31, each once within a row
- vision_rows: int32 [4, 4, 48], P('dp'), may hold values from 0 to 127, as said below
Outputs:
- merger_pre_grad: bfloat16 [768, 5120], P(('dp', 'ctx', 'mp'))
- weight_grad: float32 [5120, 4096], P(('ctx', 'mp'), 'dp')
- bias_grad: float32 [4096], P('dp')
The draws below stay inside these ranges and needn't reach their ends.
Inputs may be any that keep to these rules, and one draw needn't show every extreme that they name: `patch_counts`: each row of 4 counts sums to 24. `image_order`: each row is a permutation of the group's images. `vision_rows`: each row holds 48 distinct increasing positions, the first and last row of the shard among them.
All inputs are finite; a program needn't handle non-finite values.
Results may differ from the reference program's by a relative error of at most 0.003.
Values may be sent and summed in bfloat16 or wider, within the bound.
No kernel may reach another device: no remote copies, remote signals or barrier semaphores. Data moves between devices by JAX's collectives and lax.ppermute only.
A program may use at most 64 MiB of HBM per device.

```python
import math
import jax
import jax.numpy as jnp
import numpy as np
from jax import lax

HID = 5120
FCOL = 4096
ROWS_VIT = 24
IMG_DEV = 4
CTX_ROWS = 128
N_DP = 4
N_CTX = 4
N_MP = 2


def draw_vision_rows(key, part):
    key = jax.random.fold_in(key, 7)
    keys = jax.random.split(key, N_DP * N_CTX)
    vis_ctx = N_MP * ROWS_VIT

    def one(single):
        inner = jax.random.permutation(single, CTX_ROWS - 2)[:vis_ctx - 2].astype(jnp.int32) + 1
        picked = jnp.concatenate([jnp.zeros((1,), jnp.int32), inner, jnp.full((1,), CTX_ROWS - 1, jnp.int32)])
        return jnp.sort(picked)
    return jax.vmap(one)(keys).reshape(N_DP, N_CTX, vis_ctx)


def with_spikes(result, key, source, target, blocks, factor):
    def block_of(position):
        return (jnp.arange(result.shape[position]) // (result.shape[position] // blocks)).reshape((-1,) + (1,) * (result.ndim - 1 - position))

    first = jax.random.permutation(key, blocks)[block_of(target)]
    far = (block_of(target) + blocks // 2) % blocks
    return jnp.where((block_of(source) == first) | (block_of(source) == far), factor * result, result)


def levels(own_key, extent, cuts, low, top_value):
    def one(axis_at, parts):
        draws = jax.random.uniform(jax.random.fold_in(jax.random.fold_in(own_key, 6), axis_at), (parts,), jnp.float32, low / len(cuts), top_value / len(cuts))
        return jnp.repeat(jnp.exp(draws), extent[axis_at] // parts).reshape((-1,) + (1,) * (len(extent) - axis_at - 1))

    gain = one(*cuts[0])
    for cut in cuts[1:]:
        gain = gain * one(*cut)
    return gain


def length_profile(number_of, total, bound, skew):
    portions = [(1 << 20) // math.isqrt(grade ** skew) + 1 for grade in range(2, number_of + 1)]
    surplus, given = total - bound - (number_of - 1), [1] * (number_of - 1)
    while surplus > 0:
        candidates = [i for i in range(number_of - 1) if given[i] < bound]
        mass, remaining = sum([portions[i] for i in candidates]), surplus
        for i in candidates:
            more = min(bound - given[i], max(1, remaining * portions[i] // mass), surplus)
            given[i] = given[i] + more
            surplus = surplus - more
    return np.array([bound] + given)


def uneven_parts(key, number_of, total, limit, lean):
    if number_of == 2:
        one = jax.random.randint(key, (), max(1, total - limit), min(limit, total - 1) + 1)
        return jnp.stack([one, total - one])
    lengths = jnp.asarray(length_profile(number_of, total, limit, lean), jnp.int32)
    twos = (number_of - 1) // 2
    giver, taker = lengths[1:1 + 2 * twos:2], lengths[2:2 + 2 * twos:2]
    room = jnp.minimum(giver - 1, limit - taker)
    moved = jax.random.randint(jax.random.fold_in(key, 1), (twos,), 0, 1 << 20) % (room + 1)
    lengths = lengths.at[1:1 + 2 * twos:2].set(giver - moved).at[2:2 + 2 * twos:2].set(taker + moved)
    return lengths[jax.random.permutation(jax.random.fold_in(key, 2), number_of)]


def noise(rng, extent, spread, limit, cuts=(), held_as=jnp.bfloat16):
    gain = levels(rng, extent, cuts, -0.22, 0.18) if cuts else 1.0
    result = jax.random.normal(rng, extent, jnp.float32) * spread * gain
    return jnp.minimum(jnp.maximum(result, -limit), limit).astype(held_as)


def noise_with(key, dims, scale, most, cuts, heavy, held_as=jnp.bfloat16):
    entries = scale * jax.random.normal(key, dims, jnp.float32)
    if cuts:
        entries = entries * levels(key, dims, cuts, -0.22, 0.18)
    return jnp.clip(with_spikes(entries, jax.random.fold_in(key, 3), *heavy), -most, most).astype(held_as)


def setup_inputs(seed: int = 0) -> dict:
    arg_keys = jax.random.split(jax.random.key(seed), 7)
    llm_grad = noise_with(arg_keys[0], (N_DP * N_CTX * CTX_ROWS, FCOL), 1.0, 6.0, ((0, 16),), (0, 1, 16, 2.0))
    merger_pre = noise(arg_keys[1], (N_DP * N_CTX * N_MP * ROWS_VIT, HID), 1.0, 6.0, ((0, 32),))
    out_weight = noise(arg_keys[2], (HID, FCOL), HID ** -0.5, 0.078125, ((0, 8),))
    patch_counts = jax.vmap(lambda own: uneven_parts(own, IMG_DEV, ROWS_VIT, ROWS_VIT // 2, 2))(jax.random.split(arg_keys[3], N_DP * (N_CTX * N_MP))).reshape((N_DP, N_CTX * N_MP, IMG_DEV)).astype(jnp.int32)
    image_order = jax.vmap(lambda own: jax.random.permutation(own, N_CTX * N_MP * IMG_DEV))(jax.random.split(arg_keys[4], N_DP)).reshape((N_DP, N_CTX * N_MP * IMG_DEV)).astype(jnp.int32)
    vision_rows = draw_vision_rows(jax.random.fold_in(arg_keys[6], 71), 0)
    return dict(llm_grad=llm_grad, merger_pre=merger_pre, out_weight=out_weight, patch_counts=patch_counts, image_order=image_order, vision_rows=vision_rows)


def gelu_parts(x):
    cdf = 0.5 * (1.0 + lax.erf(x * 0.7071067811865476))
    pdf = jnp.exp(-0.5 * x * x) * 0.3989422804014327
    return x * cdf, cdf + x * pdf


def stream_index(counts, order):
    total = counts.shape[0]
    vit_end = jnp.cumsum(counts).astype(jnp.int32)
    vit_start = vit_end - counts
    onehot = (order[:, None] == jnp.arange(total, dtype=jnp.int32)[None, :]).astype(jnp.int32)
    ordered = jnp.sum(onehot * counts[None, :], axis=1).astype(jnp.int32)
    place_start = (jnp.cumsum(ordered) - ordered).astype(jnp.int32)
    llm_start = jnp.sum(onehot * place_start[:, None], axis=0).astype(jnp.int32)
    rows_all = jnp.sum(counts).astype(jnp.int32)
    return rows_all, vit_start, vit_end, llm_start - vit_start


def stream_rows(counts, order, length):
    rows_all, vit_start, vit_end, shift = stream_index(counts, order)
    rows = jnp.arange(length, dtype=jnp.int32)
    member = (rows[:, None] >= vit_start[None, :]) & (rows[:, None] < vit_end[None, :])
    return (rows + jnp.sum(jnp.where(member, shift[None, :], 0), axis=1)).astype(jnp.int32)


def reference(llm_grad, merger_pre, out_weight, patch_counts, image_order, vision_rows):
    group_rows = N_CTX * N_MP * ROWS_VIT
    vis_ctx = N_MP * ROWS_VIT
    g_groups = llm_grad.reshape(N_DP, N_CTX * CTX_ROWS, FCOL)
    u_groups = merger_pre.reshape(N_DP, group_rows, HID)

    def one(carry, items):
        g_all, pre, counts, order, places = items
        stream = stream_rows(counts.reshape(-1), order, group_rows)
        shard = stream // vis_ctx
        slot = stream % vis_ctx
        flat_places = places.reshape(-1)
        picked = (shard * CTX_ROWS + flat_places[shard * vis_ctx + slot]).astype(jnp.int32)
        row_grad = g_all[picked]
        value, slope = gelu_parts(pre.astype(jnp.float32))
        act = value.astype(jnp.bfloat16)
        act_grad = lax.dot_general(row_grad, out_weight, (((1,), (1,)), ((), ())), preferred_element_type=jnp.float32)
        pre_grad = (act_grad * slope).astype(jnp.bfloat16)
        term = lax.dot_general(act, row_grad, (((0,), (0,)), ((), ())), preferred_element_type=jnp.float32)
        bias_term = jnp.sum(row_grad.astype(jnp.float32), axis=0)
        return (carry[0] + term, carry[1] + bias_term), pre_grad

    init = (jnp.zeros((HID, FCOL), jnp.float32), jnp.zeros((FCOL,), jnp.float32))
    sums, grads = lax.scan(one, init, (g_groups, u_groups, patch_counts, image_order, vision_rows))
    return grads.reshape(N_DP * group_rows, HID), sums[0], sums[1]
```

```python
import functools

import jax
import jax.numpy as jnp
from jax import lax
from jax.experimental import pallas as pl
from jax.experimental.pallas import tpu as pltpu
from jax.sharding import PartitionSpec as P

BF16 = jnp.bfloat16
F32 = jnp.float32
VMEM = pl.BlockSpec(memory_space=pltpu.VMEM)
ANY = pl.BlockSpec(memory_space=pl.ANY)


def gelu_parts(x):
    cdf = 0.5 * (1.0 + lax.erf(x * 0.7071067811865476))
    pdf = jnp.exp(-0.5 * x * x) * 0.3989422804014327
    return (x * cdf, cdf + x * pdf)


def stream_rows(counts, order, length):
    total = counts.shape[0]
    vit_end = jnp.cumsum(counts)
    vit_start = vit_end - counts
    onehot = (order[:, None] == jnp.arange(total, dtype=jnp.int32)[None, :]).astype(jnp.int32)
    ordered = jnp.sum(onehot * counts[None, :], axis=1)
    place_start = jnp.cumsum(ordered) - ordered
    llm_start = jnp.sum(onehot * place_start[:, None], axis=0)
    shift = llm_start - vit_start
    rows = jnp.arange(length, dtype=jnp.int32)
    member = (rows[:, None] >= vit_start[None, :]) & (rows[:, None] < vit_end[None, :])
    return rows + jnp.sum(jnp.where(member, shift[None, :], 0), axis=1)


def reduced(llm_grad, merger_pre, out_weight, patch_counts, image_order, vision_rows):
    group_rows = merger_pre.shape[0] * lax.axis_size(("ctx", "mp"))
    stream = stream_rows(patch_counts.reshape(-1), image_order.reshape(-1), group_rows)
    own_places = vision_rows[0][lax.axis_index("ctx")]
    own_rows = llm_grad[own_places]
    stream_grad = lax.all_gather(own_rows, "ctx", axis=0, tiled=True)
    pre_cols = lax.all_to_all(merger_pre, ("ctx", "mp"), split_axis=1, concat_axis=0, tiled=True)
    row_grad = stream_grad[stream]
    value, slope = gelu_parts(pre_cols.astype(F32))
    act = value.astype(BF16)
    act_grad = lax.dot_general(row_grad, out_weight, (((1,), (1,)), ((), ())), preferred_element_type=F32)
    pre_grad = (act_grad * slope).astype(BF16)
    returned = lax.all_to_all(pre_grad, ("ctx", "mp"), split_axis=0, concat_axis=1, tiled=True)
    term = lax.dot_general(act, row_grad, (((0,), (0,)), ((), ())), preferred_element_type=F32)
    ones_row = jnp.ones((row_grad.shape[0],), BF16)
    bias_term = jnp.dot(ones_row, row_grad, preferred_element_type=F32)
    return (
        returned,
        lax.psum_scatter(term, "dp", scatter_dimension=1, tiled=True),
        lax.psum_scatter(bias_term, "dp", scatter_dimension=0, tiled=True),
    )


def pick_kernel(n_dp, ids, llm, places, pre, blocks, mine, other, parts, chosen):
    ctx, core = ids[1], ids[2]
    wide = blocks.shape[2]
    for i in range(blocks.shape[0]):
        blocks[i] = pre[:, i * wide : (i + 1) * wide]
    own = places[0, pl.ds(ctx, 1), :]
    hot = (lax.broadcasted_iota(jnp.int32, (llm.shape[0], own.shape[1]), 0) == own).astype(BF16)
    chosen[...] = lax.dot_general(hot, llm[...], (((0,), (0,)), ((), ())), preferred_element_type=F32).astype(BF16)
    half = mine.shape[1]
    mine[...] = chosen[:, pl.ds(pl.multiple_of(core * half, half), half)]
    other[...] = chosen[:, pl.ds(pl.multiple_of((1 - core) * half, half), half)]
    part = parts.shape[2]
    for i in range(n_dp):
        parts[i] = chosen[:, pl.ds(pl.multiple_of((2 * i + core) * part, part), part)]


def order_kernel(n_ctx, ids, counts, order, there, back):
    ctx = ids[1]
    images, rows = counts.shape[1], there.shape[0]
    block = rows // n_ctx
    up = lax.broadcasted_iota(jnp.int32, (images, images), 0)
    along = lax.broadcasted_iota(jnp.int32, (images, images), 1)
    count_row, order_row = counts[...], order[...]

    def total(mask, values, axis):
        return jnp.sum(jnp.where(mask, values, 0).astype(F32), axis=axis, keepdims=True).astype(jnp.int32)

    same = up == along
    count_col = total(same, count_row, 1)
    order_col = total(same, order_row, 1)
    vit_start_row = total(up < along, count_col, 0)
    vit_start_col = total(along < up, count_row, 1)
    placed_row = total(order_row == up, count_col, 0)
    placed_col = total(order_col == along, count_row, 1)
    place_start_col = total(along < up, placed_row, 1)
    place_start_row = total(up < along, placed_col, 0)
    llm_start_row = total(order_col == along, place_start_col, 0)
    llm_start_col = total(order_row == up, place_start_row, 1)

    def received(shape, dim):
        at = lax.broadcasted_iota(jnp.int32, shape, dim)
        out = jnp.zeros(shape, jnp.int32)
        for k in range(n_ctx):
            inside = (at >= k * block) & (at < (k + 1) * block)
            out = jnp.where(inside, at + ((ctx ^ k) - k) * block, out)
        return out

    image = lax.broadcasted_iota(jnp.int32, (rows, images), 0)
    member = (image >= vit_start_row) & (image < vit_start_row + count_row)
    stream_col = lax.broadcasted_iota(jnp.int32, (rows, 1), 0) + total(member, llm_start_row - vit_start_row, 1)
    back[...] = (stream_col == received((1, rows), 1)).astype(F32).astype(BF16)
    image = lax.broadcasted_iota(jnp.int32, (images, rows), 1)
    member = (image >= vit_start_col) & (image < vit_start_col + count_col)
    stream_row = lax.broadcasted_iota(jnp.int32, (1, rows), 1) + total(member, llm_start_col - vit_start_col, 0)
    there[...] = (stream_row == received((rows, 1), 0)).astype(F32).astype(BF16)


def act_kernel(there, pre, act, slope):
    x = jnp.dot(there[...], pre[...], preferred_element_type=F32)
    value, grade = gelu_parts(x)
    act[...] = value.astype(BF16)
    slope[...] = grade


def grad_kernel(n_ctx, ids, *refs):
    near, far = refs[:n_ctx], refs[n_ctx : 2 * n_ctx]
    weight, slope, back, out, rows, sems = refs[2 * n_ctx :]
    core = ids[2]
    block, half = near[0].shape

    @pl.when(pl.program_id(0) == 0)
    def _():
        copies = []
        for side, pieces in ((core, near), (1 - core, far)):
            at = pl.ds(pl.multiple_of(side * half, half), half)
            for k in range(n_ctx):
                copies.append(
                    pltpu.make_async_copy(pieces[k], rows.at[k * block : (k + 1) * block, at], sems.at[len(copies)])
                )
        for copy in copies:
            copy.start()
        for copy in copies:
            copy.wait()

    grad = lax.dot_general(rows[...], weight[...], (((1,), (1,)), ((), ())), preferred_element_type=F32)
    grad = (grad * slope[...]).astype(BF16)
    out[...] = jnp.dot(back[...], grad, preferred_element_type=F32).astype(BF16)


def weight_kernel(n_dp, n_ctx, ids, *refs):
    acts, near, far = refs[:n_dp], refs[n_dp : n_dp + n_ctx], refs[n_dp + n_ctx : n_dp + 2 * n_ctx]
    out, bias, left, right, sems = refs[n_dp + 2 * n_ctx :]
    group, core = ids[0], ids[2]
    rows, half = near[0].shape
    block = rows // n_dp

    @pl.when(pl.program_id(0) == 0)
    def _():
        copies = []
        for side, pieces in ((core, near), (1 - core, far)):
            at = pl.ds(pl.multiple_of(side * half, half), half)
            for k in range(n_ctx):
                copies.append(
                    pltpu.make_async_copy(pieces[k], right.at[k * rows : (k + 1) * rows, at], sems.at[len(copies)])
                )
        for j in range(n_dp):
            for k in range(n_ctx):
                to = pl.ds(pl.multiple_of((k * n_dp + (group ^ j)) * block, block), block)
                copies.append(
                    pltpu.make_async_copy(acts[j].at[k * block : (k + 1) * block], left.at[to], sems.at[len(copies)])
                )
        for copy in copies:
            copy.start()
        for copy in copies:
            copy.wait()

    wide = out.shape[1]
    piece = right[:, pl.ds(pl.multiple_of(pl.program_id(0) * wide, wide), wide)]
    out[...] = lax.dot_general(left[...], piece, (((0,), (0,)), ((), ())), preferred_element_type=F32)
    ones = jnp.ones((8, piece.shape[0]), BF16)
    bias[...] = jnp.dot(ones, piece, preferred_element_type=F32)[:1]


def struct(shape, dtype=BF16):
    return jax.ShapeDtypeStruct(shape, dtype)


def swap(x, axis, k):
    n = lax.axis_size(axis)
    return lax.ppermute(x, axis, [(i, i ^ k) for i in range(n)])


def gathered(llm_grad, merger_pre, out_weight, patch_counts, image_order, vision_rows):
    n_dp, n_ctx, n_mp = lax.axis_size("dp"), lax.axis_size("ctx"), lax.axis_size("mp")
    images = n_ctx * n_mp
    vit, hidden = merger_pre.shape
    hid, feat = out_weight.shape
    block = vision_rows.shape[-1]
    rows = n_ctx * block
    cols = feat // n_dp
    ids = jnp.stack([lax.axis_index(a) for a in ("dp", "ctx", "mp")]).astype(jnp.int32)
    smem = pl.BlockSpec(memory_space=pltpu.SMEM)

    blocks, mine, other, parts = pl.pallas_call(
        functools.partial(pick_kernel, n_dp),
        out_shape=(
            struct((images, vit, hid)),
            struct((block, feat // 2)),
            struct((block, feat // 2)),
            struct((n_dp, block, cols // 2)),
        ),
        in_specs=[smem, VMEM, VMEM, VMEM],
        out_specs=(VMEM,) * 4,
        scratch_shapes=[pltpu.VMEM((block, feat), BF16)],
        name="pick",
    )(ids, llm_grad, vision_rows, merger_pre)

    pre = lax.all_to_all(blocks, ("ctx", "mp"), 0, 0, tiled=True).reshape(rows, hid)
    split = lax.all_to_all(parts, "dp", 0, 0, tiled=True).reshape(n_dp * block, cols // 2)
    near = [mine] + [swap(mine, "ctx", k) for k in range(1, n_ctx)]
    far = [other] + [swap(x, "mp", 1) for x in near[1:]]

    there, back = pl.pallas_call(
        functools.partial(order_kernel, n_ctx),
        out_shape=(struct((rows, rows)),) * 2,
        in_specs=[smem, VMEM, VMEM],
        out_specs=(VMEM,) * 2,
        name="order",
    )(ids, patch_counts.reshape(1, -1), image_order)

    act, slope = pl.pallas_call(
        act_kernel,
        out_shape=(struct((rows, hid)), struct((rows, hid), F32)),
        in_specs=[VMEM] * 2,
        out_specs=(VMEM,) * 2,
        name="act",
    )(there, pre)
    acts = [act] + [swap(act, "dp", k) for k in range(1, n_dp)]
    near_part = [split] + [swap(split, "ctx", k) for k in range(1, n_ctx)]
    far_part = [swap(x, "mp", 1) for x in near_part]

    wide = 128
    grad = pl.pallas_call(
        functools.partial(grad_kernel, n_ctx),
        out_shape=struct((rows, hid)),
        grid=(hid // wide,),
        in_specs=[smem]
        + [ANY] * (2 * n_ctx)
        + [
            pl.BlockSpec((wide, feat), lambda i: (i, 0)),
            pl.BlockSpec((rows, wide), lambda i: (0, i)),
            pl.BlockSpec((rows, rows), lambda i: (0, 0)),
        ],
        out_specs=pl.BlockSpec((rows, wide), lambda i: (0, i)),
        scratch_shapes=[pltpu.VMEM((rows, feat), BF16), pltpu.SemaphoreType.DMA((2 * n_ctx,))],
        name="grad",
    )(ids, *near, *far, out_weight, slope, back)
    returned = lax.all_to_all(grad.reshape(images, vit, hid), ("ctx", "mp"), 0, 0, tiled=True)
    returned = jnp.swapaxes(returned, 0, 1).reshape(vit, hidden)

    wide = 256
    weight_grad, bias_grad = pl.pallas_call(
        functools.partial(weight_kernel, n_dp, n_ctx),
        out_shape=(struct((hid, cols), F32), struct((1, cols), F32)),
        grid=(cols // wide,),
        in_specs=[smem] + [ANY] * (n_dp + 2 * n_ctx),
        out_specs=(pl.BlockSpec((hid, wide), lambda i: (0, i)), pl.BlockSpec((1, wide), lambda i: (0, i))),
        scratch_shapes=[
            pltpu.VMEM((n_dp * rows, hid), BF16),
            pltpu.VMEM((n_dp * rows, cols), BF16),
            pltpu.SemaphoreType.DMA((2 * n_ctx + n_dp * n_ctx,)),
        ],
        name="weight",
    )(ids, *acts, *near_part, *far_part)
    return (returned, weight_grad, bias_grad.reshape(-1))


def solution(mesh):
    n_dp, n_ctx, n_mp = (mesh.shape[a] for a in ("dp", "ctx", "mp"))
    placed = (
        P(("dp", "ctx"), None),
        P(("dp", "ctx", "mp"), None),
        P(("ctx", "mp"), None),
        P("dp", None, None),
        P("dp", None),
        P("dp", None, None),
    )

    def per_device(*args):
        hid, feat = args[2].shape
        rows = args[1].shape[0] * n_ctx * n_mp
        gather = (n_dp - 1) * rows * (hid + feat // n_dp) * 2
        scatter = hid * feat * 4 * (n_dp - 1) // n_dp
        fits = n_mp == 2 and all(n & (n - 1) == 0 for n in (n_dp, n_ctx))
        return (gathered if fits and gather < scatter else reduced)(*args)

    return jax.shard_map(
        per_device,
        mesh=mesh,
        in_specs=placed,
        out_specs=(P(("dp", "ctx", "mp"), None), P(("ctx", "mp"), "dp"), P("dp")),
        check_vma=False,
    )
```

```python
import functools

import jax
import jax.numpy as jnp
from jax import lax
from jax.experimental import pallas as pl
from jax.experimental.pallas import tpu as pltpu
from jax.sharding import PartitionSpec as P

BF16 = jnp.bfloat16
F32 = jnp.float32
VMEM = pl.BlockSpec(memory_space=pltpu.VMEM)
ANY = pl.BlockSpec(memory_space=pl.ANY)
HBM = pl.BlockSpec(memory_space=pltpu.HBM)


def gelu_parts(x):
    cdf = 0.5 * (1.0 + lax.erf(x * 0.7071067811865476))
    pdf = jnp.exp(-0.5 * x * x) * 0.3989422804014327
    return (x * cdf, cdf + x * pdf)


def stream_rows(counts, order, length):
    total = counts.shape[0]
    vit_end = jnp.cumsum(counts)
    vit_start = vit_end - counts
    onehot = (order[:, None] == jnp.arange(total, dtype=jnp.int32)[None, :]).astype(jnp.int32)
    ordered = jnp.sum(onehot * counts[None, :], axis=1)
    place_start = jnp.cumsum(ordered) - ordered
    llm_start = jnp.sum(onehot * place_start[:, None], axis=0)
    shift = llm_start - vit_start
    rows = jnp.arange(length, dtype=jnp.int32)
    member = (rows[:, None] >= vit_start[None, :]) & (rows[:, None] < vit_end[None, :])
    return rows + jnp.sum(jnp.where(member, shift[None, :], 0), axis=1)


def reduced(llm_grad, merger_pre, out_weight, patch_counts, image_order, vision_rows):
    group_rows = merger_pre.shape[0] * lax.axis_size(("ctx", "mp"))
    stream = stream_rows(patch_counts.reshape(-1), image_order.reshape(-1), group_rows)
    own_places = vision_rows[0][lax.axis_index("ctx")]
    own_rows = llm_grad[own_places]
    stream_grad = lax.all_gather(own_rows, "ctx", axis=0, tiled=True)
    pre_cols = lax.all_to_all(merger_pre, ("ctx", "mp"), split_axis=1, concat_axis=0, tiled=True)
    row_grad = stream_grad[stream]
    value, slope = gelu_parts(pre_cols.astype(F32))
    act = value.astype(BF16)
    act_grad = lax.dot_general(row_grad, out_weight, (((1,), (1,)), ((), ())), preferred_element_type=F32)
    pre_grad = (act_grad * slope).astype(BF16)
    returned = lax.all_to_all(pre_grad, ("ctx", "mp"), split_axis=0, concat_axis=1, tiled=True)
    term = lax.dot_general(act, row_grad, (((0,), (0,)), ((), ())), preferred_element_type=F32)
    ones_row = jnp.ones((row_grad.shape[0],), BF16)
    bias_term = jnp.dot(ones_row, row_grad, preferred_element_type=F32)
    return (
        returned,
        lax.psum_scatter(term, "dp", scatter_dimension=1, tiled=True),
        lax.psum_scatter(bias_term, "dp", scatter_dimension=0, tiled=True),
    )


def cut_kernel(pre, blocks, sems):
    wide = blocks.shape[2]
    copies = [
        pltpu.make_async_copy(pre.at[:, i * wide : (i + 1) * wide], blocks.at[i], sems.at[i])
        for i in range(blocks.shape[0])
    ]
    for copy in copies:
        copy.start()
    for copy in copies:
        copy.wait()


def order_maps(ctx, n_ctx, counts, order, there, back):
    images, rows = order.shape[1], there.shape[0]
    block = rows // n_ctx
    up = lax.broadcasted_iota(jnp.int32, (images, images), 0)
    along = lax.broadcasted_iota(jnp.int32, (images, images), 1)
    order_row = order[...]

    def total(mask, values, axis):
        return jnp.sum(jnp.where(mask, values, 0).astype(F32), axis=axis, keepdims=True).astype(jnp.int32)

    same = up == along
    per = counts.shape[1]
    shard = lax.broadcasted_iota(jnp.int32, (images, counts.shape[2]), 1)
    image = lax.broadcasted_iota(jnp.int32, (images, counts.shape[2]), 0)
    count_col = jnp.zeros((images, 1), jnp.int32)
    for i in range(per):
        count_col += total(image == shard * per + i, counts[0, i : i + 1, :], 1)
    count_row = total(same, count_col, 0)
    order_col = total(same, order_row, 1)
    vit_start_row = total(up < along, count_col, 0)
    vit_start_col = total(along < up, count_row, 1)
    placed_row = total(order_row == up, count_col, 0)
    placed_col = total(order_col == along, count_row, 1)
    place_start_col = total(along < up, placed_row, 1)
    place_start_row = total(up < along, placed_col, 0)
    llm_start_row = total(order_col == along, place_start_col, 0)
    llm_start_col = total(order_row == up, place_start_row, 1)

    def received(shape, dim):
        at = lax.broadcasted_iota(jnp.int32, shape, dim)
        out = jnp.zeros(shape, jnp.int32)
        for k in range(n_ctx):
            inside = (at >= k * block) & (at < (k + 1) * block)
            out = jnp.where(inside, at + ((ctx ^ k) - k) * block, out)
        return out

    image = lax.broadcasted_iota(jnp.int32, (rows, images), 0)
    member = (image >= vit_start_row) & (image < vit_start_row + count_row)
    stream_col = lax.broadcasted_iota(jnp.int32, (rows, 1), 0) + total(member, llm_start_row - vit_start_row, 1)
    back[...] = (stream_col == received((1, rows), 1)).astype(F32).astype(BF16)
    image = lax.broadcasted_iota(jnp.int32, (images, rows), 1)
    member = (image >= vit_start_col) & (image < vit_start_col + count_col)
    stream_row = lax.broadcasted_iota(jnp.int32, (1, rows), 1) + total(member, llm_start_col - vit_start_col, 0)
    there[...] = (stream_row == received((rows, 1), 0)).astype(F32).astype(BF16)


def pick_kernel(n_dp, n_ctx, *refs):
    inputs, (mine, other, there, back), parts = refs[:4], refs[4:8], refs[8 : 8 + n_dp]
    local, (chosen, sems) = refs[8 + n_dp : 12 + n_dp], refs[12 + n_dp :]
    llm, places, counts, order = local
    group, ctx, core = (lax.axis_index(a) for a in ("dp", "ctx", "mp"))
    copies = [pltpu.make_async_copy(a, b, sems.at[i]) for i, (a, b) in enumerate(zip(inputs, local))]
    for copy in copies:
        copy.start()
    for copy in copies[1:]:
        copy.wait()
    order_maps(ctx, n_ctx, counts, order, there, back)
    own = places[0, pl.ds(ctx, 1), :]
    hot = (lax.broadcasted_iota(jnp.int32, (llm.shape[0], own.shape[1]), 0) == own).astype(BF16)
    copies[0].wait()
    chosen[...] = lax.dot_general(hot, llm[...], (((0,), (0,)), ((), ())), preferred_element_type=F32).astype(BF16)
    half = mine.shape[1]
    mine[...] = chosen[:, pl.ds(pl.multiple_of(core * half, half), half)]
    other[...] = chosen[:, pl.ds(pl.multiple_of((1 - core) * half, half), half)]
    for i, part in enumerate(parts):
        wide = part.shape[1]
        part[...] = chosen[:, pl.ds(pl.multiple_of((2 * (group ^ i) + core) * wide, wide), wide)]


def act_kernel(there, pre, act, slope):
    x = jnp.dot(there[...], pre[...], preferred_element_type=F32)
    value, grade = gelu_parts(x)
    act[...] = value.astype(BF16)
    slope[...] = grade


def stack_kernel(*refs):
    parts, out = refs[:-1], refs[-1]
    rows = parts[0].shape[0]
    for i, part in enumerate(parts):
        out[i * rows : (i + 1) * rows] = part[...]


def hold_kernel(source, out, sem):
    copy = pltpu.make_async_copy(source, out, sem)
    copy.start()
    copy.wait()


def spots(core):
    return (0, 1 + core, 2 - core, 3)


def grad_kernel(mine, one, two, other, far_one, far_two, weight, slope, back, out, rows):
    core = lax.axis_index("mp")
    block, half = mine.shape

    for side, own, first, second in ((core, mine, one, two), (1 - core, other, far_one, far_two)):
        columns = pl.ds(pl.multiple_of(side * half, half), half)
        pieces = (own[...], first[...], second[:block], second[block:])
        for spot, piece in zip(spots(side), pieces):
            rows[pl.ds(pl.multiple_of(spot * block, block), block), columns] = piece

    grad = lax.dot_general(rows[...], weight[...], (((1,), (1,)), ((), ())), preferred_element_type=F32)
    grad = (grad * slope[...]).astype(BF16)
    out[...] = jnp.dot(back[...], grad, preferred_element_type=F32).astype(BF16)


def early_kernel(n_dp, pair, two, far_pair, far_two, act, right, total, bias):
    core = lax.axis_index("mp")
    rows, half = pair.shape[0] // 2, pair.shape[1]
    block = rows // n_dp
    for side, first, second in ((core, pair, two), (1 - core, far_pair, far_two)):
        columns = pl.ds(pl.multiple_of(side * half, half), half)
        for at, spot in enumerate(spots(side)):
            piece = (first, second)[at // 2]
            for i in range(n_dp):
                to = (i * len(spots(0)) + spot) * block
                start = (at % 2) * rows + i * block
                right[pl.ds(pl.multiple_of(to, block), block), columns] = piece[start : start + block]
    ones = jnp.ones((8, right.shape[0]), BF16)
    bias[...] = jnp.dot(ones, right[...], preferred_element_type=F32)[:1]
    total[...] = lax.dot_general(
        act[...], right[: act.shape[0]], (((0,), (0,)), ((), ())), preferred_element_type=F32
    )


def late_kernel(*refs):
    acts, (right, total, out) = refs[:-3], refs[-3:]
    wide, rows = out.shape[1], acts[0].shape[0]
    at = pl.ds(pl.multiple_of(pl.program_id(0) * wide, wide), wide)
    sums = total[:, at]
    for i, act in enumerate(acts):
        piece = right[(i + 1) * rows : (i + 2) * rows, at]
        sums += lax.dot_general(act[...], piece, (((0,), (0,)), ((), ())), preferred_element_type=F32)
    out[...] = sums


def struct(shape, dtype=BF16):
    return jax.ShapeDtypeStruct(shape, dtype)


def limits(mebibytes):
    return dict(
        compiler_params=pltpu.CompilerParams(vmem_limit_bytes=mebibytes << 20),
        cost_estimate=pl.CostEstimate(flops=COST, bytes_accessed=COST, transcendentals=0),
    )


COST = 1


def swap(x, axis, k):
    n = lax.axis_size(axis)
    return lax.ppermute(x, axis, [(i, i ^ k) for i in range(n)])


def round_plane(x, step):
    pairs = [(2 * c + m, 2 * (c ^ (1 << (m ^ step))) + m) for c in range(4) for m in range(2)]
    return lax.ppermute(x, ("ctx", "mp"), pairs)


def pinned(x):
    return pltpu.with_memory_space_constraint(x, pltpu.HBM)


def stacked(parts, name):
    return pl.pallas_call(
        stack_kernel,
        out_shape=struct((len(parts) * parts[0].shape[0], parts[0].shape[1])),
        in_specs=[VMEM] * len(parts),
        out_specs=VMEM,
        name=name,
        **limits(4),
    )(*parts)


def gathered(llm_grad, merger_pre, out_weight, patch_counts, image_order, vision_rows):
    n_dp, n_ctx, n_mp = lax.axis_size("dp"), lax.axis_size("ctx"), lax.axis_size("mp")
    images = n_ctx * n_mp
    vit, hidden = merger_pre.shape
    hid, feat = out_weight.shape
    block = vision_rows.shape[-1]
    rows = n_ctx * block
    cols = feat // n_dp

    blocks = pl.pallas_call(
        cut_kernel,
        out_shape=struct((images, vit, hid)),
        in_specs=[ANY],
        out_specs=ANY,
        scratch_shapes=[pltpu.SemaphoreType.DMA((images,))],
        name="cut",
        **limits(4),
    )(merger_pre)
    llm_grad, blocks = lax.optimization_barrier((llm_grad, blocks))
    pre = lax.all_to_all(blocks, ("ctx", "mp"), 0, 0, tiled=True).reshape(rows, hid)

    inputs = (llm_grad, vision_rows, jnp.swapaxes(patch_counts, 1, 2), image_order)
    mine, other, there, back, *parts = pl.pallas_call(
        functools.partial(pick_kernel, n_dp, n_ctx),
        out_shape=(struct((block, feat // 2)),) * 2
        + (struct((rows, rows)),) * 2
        + (struct((block, cols // 2)),) * n_dp,
        in_specs=[HBM] * 4,
        out_specs=(VMEM,) * (4 + n_dp),
        scratch_shapes=[pltpu.VMEM(x.shape, x.dtype) for x in inputs]
        + [pltpu.VMEM((block, feat), BF16), pltpu.SemaphoreType.DMA((4,))],
        name="pick",
        **limits(8),
    )(*(pinned(x) for x in inputs))

    parts = [parts[0]] + [swap(parts[k], "dp", k) for k in range(1, n_dp)]
    one = round_plane(mine, 0)
    pre, *parts = lax.optimization_barrier((pre, *parts))
    act, slope = pl.pallas_call(
        act_kernel,
        out_shape=(struct((rows, hid)), struct((rows, hid), F32)),
        in_specs=[VMEM] * 2,
        out_specs=(VMEM,) * 2,
        name="act",
        **limits(4),
    )(there, pre)
    acts = {0: act} | {k: swap(act, "dp", k) for k in range(1, n_dp) if k & (k - 1) == 0}
    out_weight, one, _ = lax.optimization_barrier((out_weight, one, act))
    two = round_plane(stacked((mine, one), "pair"), 1)
    held = pl.pallas_call(
        hold_kernel,
        out_shape=struct(out_weight.shape),
        in_specs=[HBM],
        out_specs=VMEM,
        scratch_shapes=[pltpu.SemaphoreType.DMA],
        name="hold",
        **limits(8),
    )(pinned(out_weight))

    split = stacked(parts, "parts")
    one_part = round_plane(split, 0)
    one, two, held, split, one_part = lax.optimization_barrier((one, two, held, split, one_part))
    far_one, far_two = swap(one, "mp", 1), swap(two, "mp", 1)
    pair = stacked((split, one_part), "pair_part")
    far_pair = swap(pair, "mp", 1)
    two_part = round_plane(pair, 1)
    far_two_part = swap(two_part, "mp", 1)

    grad = pl.pallas_call(
        grad_kernel,
        out_shape=struct((rows, hid)),
        in_specs=[VMEM] * 9,
        out_specs=VMEM,
        scratch_shapes=[pltpu.VMEM((rows, feat), BF16)],
        name="grad",
        **limits(8),
    )(mine, one, two, other, far_one, far_two, held, slope, back)
    relay, _ = lax.optimization_barrier(([acts[k] for k in sorted(acts)], grad))
    relay = dict(zip(sorted(acts), relay))
    for k in range(n_dp):
        if k not in acts:
            acts[k] = swap(relay[k ^ (k & -k)] if k ^ (k & -k) in relay else acts[k ^ (k & -k)], "dp", k & -k)
    returned = lax.all_to_all(grad.reshape(images, vit, hid), ("ctx", "mp"), 0, 0, tiled=True)

    right, total, bias_grad = pl.pallas_call(
        functools.partial(early_kernel, n_dp),
        out_shape=(struct((n_dp * rows, cols)), struct((hid, cols), F32), struct((1, cols), F32)),
        in_specs=[VMEM] * 5,
        out_specs=(VMEM,) * 3,
        name="early",
        **limits(12),
    )(pair, two_part, far_pair, far_two_part, act)
    wide = cols // 2
    weight_grad = pl.pallas_call(
        late_kernel,
        out_shape=struct((hid, cols), F32),
        grid=(cols // wide,),
        in_specs=[VMEM] * (n_dp + 1),
        out_specs=pl.BlockSpec((hid, wide), lambda i: (0, i)),
        name="late",
        **limits(12),
    )(*(acts[k] for k in range(1, n_dp)), right, total)
    returned, weight_grad = lax.optimization_barrier((returned, weight_grad))
    returned = jnp.swapaxes(returned, 0, 1).reshape(vit, hidden)
    return (returned, weight_grad, bias_grad.reshape(-1))


def solution(mesh):
    n_dp, n_ctx, n_mp = (mesh.shape[a] for a in ("dp", "ctx", "mp"))
    placed = (
        P(("dp", "ctx"), None),
        P(("dp", "ctx", "mp"), None),
        P(("ctx", "mp"), None),
        P("dp", None, None),
        P("dp", None),
        P("dp", None, None),
    )

    def per_device(*args):
        hid, feat = args[2].shape
        rows = args[1].shape[0] * n_ctx * n_mp
        gather = (n_dp - 1) * rows * (hid + feat // n_dp) * 2
        scatter = hid * feat * 4 * (n_dp - 1) // n_dp
        fits = n_mp == 2 and n_ctx == 4 and n_dp & (n_dp - 1) == 0 and n_dp > 1
        return (gathered if fits and gather < scatter else reduced)(*args)

    return jax.shard_map(
        per_device,
        mesh=mesh,
        in_specs=placed,
        out_specs=(P(("dp", "ctx", "mp"), None), P(("ctx", "mp"), "dp"), P("dp")),
        check_vma=False,
    )
```

```python
import functools

import jax
import jax.numpy as jnp
from jax import lax
from jax.experimental import pallas as pl
from jax.experimental.pallas import tpu as pltpu
from jax.sharding import PartitionSpec as P

BF16 = jnp.bfloat16
F32 = jnp.float32
VMEM = pl.BlockSpec(memory_space=pltpu.VMEM)
ANY = pl.BlockSpec(memory_space=pl.ANY)
HBM = pl.BlockSpec(memory_space=pltpu.HBM)


def gelu_parts(x):
    cdf = 0.5 * (1.0 + lax.erf(x * 0.7071067811865476))
    pdf = jnp.exp(-0.5 * x * x) * 0.3989422804014327
    return (x * cdf, cdf + x * pdf)


def stream_rows(counts, order, length):
    total = counts.shape[0]
    vit_end = jnp.cumsum(counts)
    vit_start = vit_end - counts
    onehot = (order[:, None] == jnp.arange(total, dtype=jnp.int32)[None, :]).astype(jnp.int32)
    ordered = jnp.sum(onehot * counts[None, :], axis=1)
    place_start = jnp.cumsum(ordered) - ordered
    llm_start = jnp.sum(onehot * place_start[:, None], axis=0)
    shift = llm_start - vit_start
    rows = jnp.arange(length, dtype=jnp.int32)
    member = (rows[:, None] >= vit_start[None, :]) & (rows[:, None] < vit_end[None, :])
    return rows + jnp.sum(jnp.where(member, shift[None, :], 0), axis=1)


def reduced(llm_grad, merger_pre, out_weight, patch_counts, image_order, vision_rows):
    group_rows = merger_pre.shape[0] * lax.axis_size(("ctx", "mp"))
    stream = stream_rows(patch_counts.reshape(-1), image_order.reshape(-1), group_rows)
    own_places = vision_rows[0][lax.axis_index("ctx")]
    own_rows = llm_grad[own_places]
    stream_grad = lax.all_gather(own_rows, "ctx", axis=0, tiled=True)
    pre_cols = lax.all_to_all(merger_pre, ("ctx", "mp"), split_axis=1, concat_axis=0, tiled=True)
    row_grad = stream_grad[stream]
    value, slope = gelu_parts(pre_cols.astype(F32))
    act = value.astype(BF16)
    act_grad = lax.dot_general(row_grad, out_weight, (((1,), (1,)), ((), ())), preferred_element_type=F32)
    pre_grad = (act_grad * slope).astype(BF16)
    returned = lax.all_to_all(pre_grad, ("ctx", "mp"), split_axis=0, concat_axis=1, tiled=True)
    term = lax.dot_general(act, row_grad, (((0,), (0,)), ((), ())), preferred_element_type=F32)
    ones_row = jnp.ones((row_grad.shape[0],), BF16)
    bias_term = jnp.dot(ones_row, row_grad, preferred_element_type=F32)
    return (
        returned,
        lax.psum_scatter(term, "dp", scatter_dimension=1, tiled=True),
        lax.psum_scatter(bias_term, "dp", scatter_dimension=0, tiled=True),
    )


def cut_kernel(pre, blocks, sems):
    wide = blocks.shape[2]
    copies = [
        pltpu.make_async_copy(pre.at[:, i * wide : (i + 1) * wide], blocks.at[i], sems.at[i])
        for i in range(blocks.shape[0])
    ]
    for copy in copies:
        copy.start()
    for copy in copies:
        copy.wait()


def order_maps(ctx, n_ctx, counts, order, there, back):
    images, rows = order.shape[1], there.shape[0]
    block = rows // n_ctx
    up = lax.broadcasted_iota(jnp.int32, (images, images), 0)
    along = lax.broadcasted_iota(jnp.int32, (images, images), 1)
    order_row = order[...]

    def total(mask, values, axis):
        return jnp.sum(jnp.where(mask, values, 0).astype(F32), axis=axis, keepdims=True).astype(jnp.int32)

    same = up == along
    per = counts.shape[1]
    shard = lax.broadcasted_iota(jnp.int32, (images, counts.shape[2]), 1)
    image = lax.broadcasted_iota(jnp.int32, (images, counts.shape[2]), 0)
    count_col = jnp.zeros((images, 1), jnp.int32)
    for i in range(per):
        count_col += total(image == shard * per + i, counts[0, i : i + 1, :], 1)
    count_row = total(same, count_col, 0)
    order_col = total(same, order_row, 1)
    vit_start_row = total(up < along, count_col, 0)
    vit_start_col = total(along < up, count_row, 1)
    placed_row = total(order_row == up, count_col, 0)
    placed_col = total(order_col == along, count_row, 1)
    place_start_col = total(along < up, placed_row, 1)
    place_start_row = total(up < along, placed_col, 0)
    llm_start_row = total(order_col == along, place_start_col, 0)
    llm_start_col = total(order_row == up, place_start_row, 1)

    def received(shape, dim):
        at = lax.broadcasted_iota(jnp.int32, shape, dim)
        out = jnp.zeros(shape, jnp.int32)
        for k in range(n_ctx):
            inside = (at >= k * block) & (at < (k + 1) * block)
            out = jnp.where(inside, at + ((ctx ^ k) - k) * block, out)
        return out

    image = lax.broadcasted_iota(jnp.int32, (rows, images), 0)
    member = (image >= vit_start_row) & (image < vit_start_row + count_row)
    stream_col = lax.broadcasted_iota(jnp.int32, (rows, 1), 0) + total(member, llm_start_row - vit_start_row, 1)
    back[...] = (stream_col == received((1, rows), 1)).astype(F32).astype(BF16)
    image = lax.broadcasted_iota(jnp.int32, (images, rows), 1)
    member = (image >= vit_start_col) & (image < vit_start_col + count_col)
    stream_row = lax.broadcasted_iota(jnp.int32, (1, rows), 1) + total(member, llm_start_col - vit_start_col, 0)
    there[...] = (stream_row == received((rows, 1), 0)).astype(F32).astype(BF16)


def pick_kernel(n_ctx, *refs):
    inputs, (chosen, there, back), parts = refs[:4], refs[4:7], refs[7:10]
    local, sems = refs[10:14], refs[14]
    llm, places, counts, order = local
    group, ctx, core = (lax.axis_index(a) for a in ("dp", "ctx", "mp"))
    copies = [pltpu.make_async_copy(a, b, sems.at[i]) for i, (a, b) in enumerate(zip(inputs, local))]
    for copy in copies:
        copy.start()
    for copy in copies[1:]:
        copy.wait()
    order_maps(ctx, n_ctx, counts, order, there, back)
    own = places[0, pl.ds(ctx, 1), :]
    hot = (lax.broadcasted_iota(jnp.int32, (llm.shape[0], own.shape[1]), 0) == own).astype(BF16)
    copies[0].wait()
    chosen[...] = lax.dot_general(hot, llm[...], (((0,), (0,)), ((), ())), preferred_element_type=F32).astype(BF16)
    wide = parts[0].shape[1]
    for out, distances in zip(parts, ((0,), (2,), (1, 3))):
        for i, far in enumerate(distances):
            at = pl.ds(pl.multiple_of((2 * (group ^ far) + core) * wide, wide), wide)
            out[i * chosen.shape[0] : (i + 1) * chosen.shape[0]] = chosen[:, at]


def act_kernel(there, pre, act, slope):
    x = jnp.dot(there[...], pre[...], preferred_element_type=F32)
    value, grade = gelu_parts(x)
    act[...] = value.astype(BF16)
    slope[...] = grade


def stack_kernel(starts, *refs):
    parts, out = refs[:-1], refs[-1]
    at = 0
    for part, start in zip(parts, starts):
        rows = part.shape[0] - start
        out[at : at + rows] = part[start:]
        at += rows


def spread_kernel(keep, first, second, out):
    rows = keep.shape[0]
    out[:rows] = keep[...]
    out[rows : 2 * rows] = first[:rows]
    out[2 * rows :] = second[...]


def hold_kernel(source, out, sem):
    copy = pltpu.make_async_copy(source, out, sem)
    copy.start()
    copy.wait()


def grad_kernel(mine, one, two, weight, slope, back, out, rows):
    core = lax.axis_index("mp")
    block = mine.shape[0]
    pieces = (mine[...], one[...], two[:block], two[block:])
    for spot, piece in zip((0, 1 + core, 2 - core, 3), pieces):
        rows[pl.ds(pl.multiple_of(spot * block, block), block)] = piece
    grad = lax.dot_general(rows[...], weight[...], (((1,), (1,)), ((), ())), preferred_element_type=F32)
    grad = (grad * slope[...]).astype(BF16)
    out[...] = jnp.dot(back[...], grad, preferred_element_type=F32).astype(BF16)


def early_kernel(n_dp, n_ctx, *refs):
    near, far, (act, right, total, bias) = refs[:n_ctx], refs[n_ctx : 2 * n_ctx], refs[2 * n_ctx :]
    core = lax.axis_index("mp")
    rows, half = near[0].shape
    block = rows // n_dp
    for side, pieces in ((core, near), (1 - core, far)):
        columns = pl.ds(pl.multiple_of(side * half, half), half)
        for k, piece in enumerate(pieces):
            for i in range(n_dp):
                to = (i * n_ctx + k) * block
                right[to : to + block, columns] = piece[i * block : (i + 1) * block]
    ones = jnp.ones((8, right.shape[0]), BF16)
    bias[...] = jnp.dot(ones, right[...], preferred_element_type=F32)[:1]
    total[...] = lax.dot_general(
        act[...], right[: act.shape[0]], (((0,), (0,)), ((), ())), preferred_element_type=F32
    )


def late_kernel(*refs):
    acts, (right, total, out) = refs[:-3], refs[-3:]
    wide, rows = out.shape[1], acts[0].shape[0]
    at = pl.ds(pl.multiple_of(pl.program_id(0) * wide, wide), wide)
    sums = total[:, at]
    for i, act in enumerate(acts):
        piece = right[(i + 1) * rows : (i + 2) * rows, at]
        sums += lax.dot_general(act[...], piece, (((0,), (0,)), ((), ())), preferred_element_type=F32)
    out[...] = sums


def struct(shape, dtype=BF16):
    return jax.ShapeDtypeStruct(shape, dtype)


def limits(mebibytes, cost=1):
    return dict(
        compiler_params=pltpu.CompilerParams(vmem_limit_bytes=mebibytes << 20),
        cost_estimate=pl.CostEstimate(flops=cost, bytes_accessed=cost, transcendentals=0),
    )


def swap(x, axis, k):
    n = lax.axis_size(axis)
    return lax.ppermute(x, axis, [(i, i ^ k) for i in range(n)])


def pinned(x):
    return pltpu.with_memory_space_constraint(x, pltpu.HBM)


def round_plane(x, step):
    pairs = [(2 * c + m, 2 * (c ^ (1 << (m ^ step))) + m) for c in range(4) for m in range(2)]
    return lax.ppermute(x, ("ctx", "mp"), pairs)


def stacked(kernel, parts, rows, name):
    return pl.pallas_call(
        kernel,
        out_shape=struct((rows, parts[0].shape[1])),
        in_specs=[VMEM] * len(parts),
        out_specs=VMEM,
        name=name,
        **limits(4),
    )(*parts)


def gathered(llm_grad, merger_pre, out_weight, patch_counts, image_order, vision_rows):
    n_dp, n_ctx, n_mp = lax.axis_size("dp"), lax.axis_size("ctx"), lax.axis_size("mp")
    images = n_ctx * n_mp
    vit, hidden = merger_pre.shape
    hid, feat = out_weight.shape
    block = vision_rows.shape[-1]
    rows = n_ctx * block
    cols = feat // n_dp

    blocks = pl.pallas_call(
        cut_kernel,
        out_shape=struct((images, vit, hid)),
        in_specs=[ANY],
        out_specs=ANY,
        scratch_shapes=[pltpu.SemaphoreType.DMA((images,))],
        name="cut",
        **limits(4),
    )(merger_pre)
    llm_grad, blocks = lax.optimization_barrier((llm_grad, blocks))
    pre = lax.all_to_all(blocks, ("ctx", "mp"), 0, 0, tiled=True).reshape(rows, hid)

    inputs = (llm_grad, vision_rows, jnp.swapaxes(patch_counts, 1, 2), image_order)
    mine, there, back, keep, pass_on, send = pl.pallas_call(
        functools.partial(pick_kernel, n_ctx),
        out_shape=(struct((block, feat)),)
        + (struct((rows, rows)),) * 2
        + (struct((block, cols // 2)),) * 2
        + (struct((2 * block, cols // 2)),),
        in_specs=[HBM] * 4,
        out_specs=(VMEM,) * 6,
        scratch_shapes=[pltpu.VMEM(x.shape, x.dtype) for x in inputs]
        + [pltpu.SemaphoreType.DMA((4,))],
        name="pick",
        **limits(8),
    )(*(pinned(x) for x in inputs))

    one = round_plane(mine, 0)
    first = swap(send, "dp", 1)
    act, slope = pl.pallas_call(
        act_kernel,
        out_shape=(struct((rows, hid)), struct((rows, hid), F32)),
        in_specs=[VMEM] * 2,
        out_specs=(VMEM,) * 2,
        name="act",
        **limits(4, 1),
    )(there, pre)
    acts = {0: act} | {k: swap(act, "dp", k) for k in range(1, n_dp) if k & (k - 1) == 0}
    out_weight, one, first, _ = lax.optimization_barrier((out_weight, one, first, act))
    two = round_plane(stacked(functools.partial(stack_kernel, (0, 0)), (mine, one), 2 * block, "pair"), 1)
    second = stacked(functools.partial(stack_kernel, (0, block)), (pass_on, first), 2 * block, "pass_on")
    second = swap(second, "dp", 2)
    held = pl.pallas_call(
        hold_kernel,
        out_shape=struct(out_weight.shape),
        in_specs=[HBM],
        out_specs=VMEM,
        scratch_shapes=[pltpu.SemaphoreType.DMA],
        name="hold",
        **limits(8),
    )(pinned(out_weight))

    second, held = lax.optimization_barrier((second, held))
    split = stacked(spread_kernel, (keep, first, second), n_dp * block, "parts")
    near_part = [split] + [swap(split, "ctx", k) for k in range(1, n_ctx)]
    far_part = [swap(x, "mp", 1) for x in near_part]

    grad = pl.pallas_call(
        grad_kernel,
        out_shape=struct((rows, hid)),
        in_specs=[VMEM] * 6,
        out_specs=VMEM,
        scratch_shapes=[pltpu.VMEM((rows, feat), BF16)],
        name="grad",
        **limits(8),
    )(mine, one, two, held, slope, back)
    relay, _ = lax.optimization_barrier(([acts[k] for k in sorted(acts)], grad))
    relay = dict(zip(sorted(acts), relay))
    for k in range(n_dp):
        if k not in acts:
            acts[k] = swap(relay[k ^ (k & -k)] if k ^ (k & -k) in relay else acts[k ^ (k & -k)], "dp", k & -k)
    returned = lax.all_to_all(grad.reshape(images, vit, hid), ("ctx", "mp"), 0, 0, tiled=True)

    right, total, bias_grad = pl.pallas_call(
        functools.partial(early_kernel, n_dp, n_ctx),
        out_shape=(struct((n_dp * rows, cols)), struct((hid, cols), F32), struct((1, cols), F32)),
        in_specs=[VMEM] * (2 * n_ctx + 1),
        out_specs=(VMEM,) * 3,
        name="early",
        **limits(12),
    )(*near_part, *far_part, act)
    wide = cols // 2
    weight_grad = pl.pallas_call(
        late_kernel,
        out_shape=struct((hid, cols), F32),
        grid=(cols // wide,),
        in_specs=[VMEM] * (n_dp + 1),
        out_specs=pl.BlockSpec((hid, wide), lambda i: (0, i)),
        name="late",
        **limits(12),
    )(*(acts[k] for k in range(1, n_dp)), right, total)
    returned, weight_grad = lax.optimization_barrier((returned, weight_grad))
    returned = jnp.swapaxes(returned, 0, 1).reshape(vit, hidden)
    return (returned, weight_grad, bias_grad.reshape(-1))


def solution(mesh):
    n_dp, n_ctx, n_mp = (mesh.shape[a] for a in ("dp", "ctx", "mp"))
    placed = (
        P(("dp", "ctx"), None),
        P(("dp", "ctx", "mp"), None),
        P(("ctx", "mp"), None),
        P("dp", None, None),
        P("dp", None),
        P("dp", None, None),
    )

    def per_device(*args):
        hid, feat = args[2].shape
        rows = args[1].shape[0] * n_ctx * n_mp
        gather = (n_dp - 1) * rows * (hid + feat // n_dp) * 2
        scatter = hid * feat * 4 * (n_dp - 1) // n_dp
        fits = (n_dp, n_ctx, n_mp) == (4, 4, 2)
        return (gathered if fits and gather < scatter else reduced)(*args)

    return jax.shard_map(
        per_device,
        mesh=mesh,
        in_specs=placed,
        out_specs=(P(("dp", "ctx", "mp"), None), P(("ctx", "mp"), "dp"), P("dp")),
        check_vma=False,
    )
```

```python
import functools

import jax
import jax.numpy as jnp
from jax import lax
from jax.experimental import pallas as pl
from jax.experimental.pallas import tpu as pltpu
from jax.sharding import PartitionSpec as P

BF16 = jnp.bfloat16
F32 = jnp.float32
VMEM = pl.BlockSpec(memory_space=pltpu.VMEM)
ANY = pl.BlockSpec(memory_space=pl.ANY)
HBM = pl.BlockSpec(memory_space=pltpu.HBM)


def gelu_parts(x):
    cdf = 0.5 * (1.0 + lax.erf(x * 0.7071067811865476))
    pdf = jnp.exp(-0.5 * x * x) * 0.3989422804014327
    return (x * cdf, cdf + x * pdf)


def stream_rows(counts, order, length):
    total = counts.shape[0]
    vit_end = jnp.cumsum(counts)
    vit_start = vit_end - counts
    onehot = (order[:, None] == jnp.arange(total, dtype=jnp.int32)[None, :]).astype(jnp.int32)
    ordered = jnp.sum(onehot * counts[None, :], axis=1)
    place_start = jnp.cumsum(ordered) - ordered
    llm_start = jnp.sum(onehot * place_start[:, None], axis=0)
    shift = llm_start - vit_start
    rows = jnp.arange(length, dtype=jnp.int32)
    member = (rows[:, None] >= vit_start[None, :]) & (rows[:, None] < vit_end[None, :])
    return rows + jnp.sum(jnp.where(member, shift[None, :], 0), axis=1)


def reduced(llm_grad, merger_pre, out_weight, patch_counts, image_order, vision_rows):
    group_rows = merger_pre.shape[0] * lax.axis_size(("ctx", "mp"))
    stream = stream_rows(patch_counts.reshape(-1), image_order.reshape(-1), group_rows)
    own_places = vision_rows[0][lax.axis_index("ctx")]
    own_rows = llm_grad[own_places]
    stream_grad = lax.all_gather(own_rows, "ctx", axis=0, tiled=True)
    pre_cols = lax.all_to_all(merger_pre, ("ctx", "mp"), split_axis=1, concat_axis=0, tiled=True)
    row_grad = stream_grad[stream]
    value, slope = gelu_parts(pre_cols.astype(F32))
    act = value.astype(BF16)
    act_grad = lax.dot_general(row_grad, out_weight, (((1,), (1,)), ((), ())), preferred_element_type=F32)
    pre_grad = (act_grad * slope).astype(BF16)
    returned = lax.all_to_all(pre_grad, ("ctx", "mp"), split_axis=0, concat_axis=1, tiled=True)
    term = lax.dot_general(act, row_grad, (((0,), (0,)), ((), ())), preferred_element_type=F32)
    ones_row = jnp.ones((row_grad.shape[0],), BF16)
    bias_term = jnp.dot(ones_row, row_grad, preferred_element_type=F32)
    return (
        returned,
        lax.psum_scatter(term, "dp", scatter_dimension=1, tiled=True),
        lax.psum_scatter(bias_term, "dp", scatter_dimension=0, tiled=True),
    )


def cut_kernel(pre, blocks, sems):
    wide = blocks.shape[2]
    copies = [
        pltpu.make_async_copy(pre.at[:, i * wide : (i + 1) * wide], blocks.at[i], sems.at[i])
        for i in range(blocks.shape[0])
    ]
    for copy in copies:
        copy.start()
    for copy in copies:
        copy.wait()


def order_maps(ctx, n_ctx, counts, order, there, back):
    images, rows = order.shape[1], there.shape[0]
    block = rows // n_ctx
    up = lax.broadcasted_iota(jnp.int32, (images, images), 0)
    along = lax.broadcasted_iota(jnp.int32, (images, images), 1)
    order_row = order[...]

    def total(mask, values, axis):
        return jnp.sum(jnp.where(mask, values, 0).astype(F32), axis=axis, keepdims=True).astype(jnp.int32)

    same = up == along
    per = counts.shape[1]
    shard = lax.broadcasted_iota(jnp.int32, (images, counts.shape[2]), 1)
    image = lax.broadcasted_iota(jnp.int32, (images, counts.shape[2]), 0)
    count_col = jnp.zeros((images, 1), jnp.int32)
    for i in range(per):
        count_col += total(image == shard * per + i, counts[0, i : i + 1, :], 1)
    count_row = total(same, count_col, 0)
    order_col = total(same, order_row, 1)
    vit_start_row = total(up < along, count_col, 0)
    vit_start_col = total(along < up, count_row, 1)
    placed_row = total(order_row == up, count_col, 0)
    placed_col = total(order_col == along, count_row, 1)
    place_start_col = total(along < up, placed_row, 1)
    place_start_row = total(up < along, placed_col, 0)
    llm_start_row = total(order_col == along, place_start_col, 0)
    llm_start_col = total(order_row == up, place_start_row, 1)

    def received(shape, dim):
        at = lax.broadcasted_iota(jnp.int32, shape, dim)
        out = jnp.zeros(shape, jnp.int32)
        for k in range(n_ctx):
            inside = (at >= k * block) & (at < (k + 1) * block)
            out = jnp.where(inside, at + ((ctx ^ k) - k) * block, out)
        return out

    image = lax.broadcasted_iota(jnp.int32, (rows, images), 0)
    member = (image >= vit_start_row) & (image < vit_start_row + count_row)
    stream_col = lax.broadcasted_iota(jnp.int32, (rows, 1), 0) + total(member, llm_start_row - vit_start_row, 1)
    back[...] = (stream_col == received((1, rows), 1)).astype(F32).astype(BF16)
    image = lax.broadcasted_iota(jnp.int32, (images, rows), 1)
    member = (image >= vit_start_col) & (image < vit_start_col + count_col)
    stream_row = lax.broadcasted_iota(jnp.int32, (1, rows), 1) + total(member, llm_start_col - vit_start_col, 0)
    there[...] = (stream_row == received((rows, 1), 0)).astype(F32).astype(BF16)


def pick_kernel(n_ctx, *refs):
    inputs, (chosen, there, back), parts = refs[:4], refs[4:7], refs[7:10]
    local, sems = refs[10:14], refs[14]
    llm, places, counts, order = local
    group, ctx, core = (lax.axis_index(a) for a in ("dp", "ctx", "mp"))
    copies = [pltpu.make_async_copy(a, b, sems.at[i]) for i, (a, b) in enumerate(zip(inputs, local))]
    for copy in copies:
        copy.start()
    for copy in copies[1:]:
        copy.wait()
    order_maps(ctx, n_ctx, counts, order, there, back)
    own = places[0, pl.ds(ctx, 1), :]
    hot = (lax.broadcasted_iota(jnp.int32, (llm.shape[0], own.shape[1]), 0) == own).astype(BF16)
    copies[0].wait()
    chosen[...] = lax.dot_general(hot, llm[...], (((0,), (0,)), ((), ())), preferred_element_type=F32).astype(BF16)
    wide = parts[0].shape[1]
    for out, distances in zip(parts, ((0,), (2,), (1, 3))):
        for i, far in enumerate(distances):
            at = pl.ds(pl.multiple_of((2 * (group ^ far) + core) * wide, wide), wide)
            out[i * chosen.shape[0] : (i + 1) * chosen.shape[0]] = chosen[:, at]


def act_kernel(there, pre, act, slope):
    x = jnp.dot(there[...], pre[...], preferred_element_type=F32)
    value, grade = gelu_parts(x)
    act[...] = value.astype(BF16)
    slope[...] = grade


def stack_kernel(starts, *refs):
    parts, out = refs[:-1], refs[-1]
    at = 0
    for part, start in zip(parts, starts):
        rows = part.shape[0] - start
        out[at : at + rows] = part[start:]
        at += rows


def spread_kernel(keep, first, second, out):
    rows = keep.shape[0]
    out[:rows] = keep[...]
    out[rows : 2 * rows] = first[:rows]
    out[2 * rows :] = second[...]


def hold_kernel(source, out, sem):
    copy = pltpu.make_async_copy(source, out, sem)
    copy.start()
    copy.wait()


def grad_kernel(mine, one, two, weight, slope, back, out, rows):
    core = lax.axis_index("mp")
    block = mine.shape[0]
    pieces = (mine[...], one[...], two[:block], two[block:])
    for spot, piece in zip((0, 1 + core, 2 - core, 3), pieces):
        rows[pl.ds(pl.multiple_of(spot * block, block), block)] = piece
    grad = lax.dot_general(rows[...], weight[...], (((1,), (1,)), ((), ())), preferred_element_type=F32)
    grad = (grad * slope[...]).astype(BF16)
    out[...] = jnp.dot(back[...], grad, preferred_element_type=F32).astype(BF16)


def early_kernel(n_dp, n_ctx, *refs):
    near, far, (act, right, total, bias) = refs[:n_ctx], refs[n_ctx : 2 * n_ctx], refs[2 * n_ctx :]
    core = lax.axis_index("mp")
    rows, half = near[0].shape
    block = rows // n_dp
    for side, pieces in ((core, near), (1 - core, far)):
        columns = pl.ds(pl.multiple_of(side * half, half), half)
        for k, piece in enumerate(pieces):
            for i in range(n_dp):
                to = (i * n_ctx + k) * block
                right[to : to + block, columns] = piece[i * block : (i + 1) * block]
    ones = jnp.ones((8, right.shape[0]), BF16)
    bias[...] = jnp.dot(ones, right[...], preferred_element_type=F32)[:1]
    total[...] = lax.dot_general(
        act[...], right[: act.shape[0]], (((0,), (0,)), ((), ())), preferred_element_type=F32
    )


def late_kernel(*refs):
    acts, (right, total, out) = refs[:-3], refs[-3:]
    wide, rows = out.shape[1], acts[0].shape[0]
    at = pl.ds(pl.multiple_of(pl.program_id(0) * wide, wide), wide)
    sums = total[:, at]
    for i, act in enumerate(acts):
        piece = right[(i + 1) * rows : (i + 2) * rows, at]
        sums += lax.dot_general(act[...], piece, (((0,), (0,)), ((), ())), preferred_element_type=F32)
    out[...] = sums


def struct(shape, dtype=BF16):
    return jax.ShapeDtypeStruct(shape, dtype)


def limits(mebibytes, cost=1):
    return dict(
        compiler_params=pltpu.CompilerParams(vmem_limit_bytes=mebibytes << 20),
        cost_estimate=pl.CostEstimate(flops=cost, bytes_accessed=cost, transcendentals=0),
    )


def swap(x, axis, k):
    n = lax.axis_size(axis)
    return lax.ppermute(x, axis, [(i, i ^ k) for i in range(n)])


def pinned(x):
    return pltpu.with_memory_space_constraint(x, pltpu.HBM)


def round_plane(x, step):
    pairs = [(2 * c + m, 2 * (c ^ (1 << (m ^ step))) + m) for c in range(4) for m in range(2)]
    return lax.ppermute(x, ("ctx", "mp"), pairs)


def stacked(kernel, parts, rows, name):
    return pl.pallas_call(
        kernel,
        out_shape=struct((rows, parts[0].shape[1])),
        in_specs=[VMEM] * len(parts),
        out_specs=VMEM,
        name=name,
        **limits(4),
    )(*parts)


def gathered(llm_grad, merger_pre, out_weight, patch_counts, image_order, vision_rows):
    n_dp, n_ctx, n_mp = lax.axis_size("dp"), lax.axis_size("ctx"), lax.axis_size("mp")
    images = n_ctx * n_mp
    vit, hidden = merger_pre.shape
    hid, feat = out_weight.shape
    block = vision_rows.shape[-1]
    rows = n_ctx * block
    cols = feat // n_dp

    blocks = pl.pallas_call(
        cut_kernel,
        out_shape=struct((images, vit, hid)),
        in_specs=[HBM],
        out_specs=VMEM,
        scratch_shapes=[pltpu.SemaphoreType.DMA((images,))],
        name="cut",
        **limits(4),
    )(pinned(merger_pre))
    llm_grad, blocks = lax.optimization_barrier((llm_grad, blocks))
    pre = lax.all_to_all(blocks, ("ctx", "mp"), 0, 0, tiled=True).reshape(rows, hid)

    inputs = (llm_grad, vision_rows, jnp.swapaxes(patch_counts, 1, 2), image_order)
    mine, there, back, keep, pass_on, send = pl.pallas_call(
        functools.partial(pick_kernel, n_ctx),
        out_shape=(struct((block, feat)),)
        + (struct((rows, rows)),) * 2
        + (struct((block, cols // 2)),) * 2
        + (struct((2 * block, cols // 2)),),
        in_specs=[HBM] * 4,
        out_specs=(VMEM,) * 6,
        scratch_shapes=[pltpu.VMEM(x.shape, x.dtype) for x in inputs]
        + [pltpu.SemaphoreType.DMA((4,))],
        name="pick",
        **limits(8),
    )(*(pinned(x) for x in inputs))

    one = round_plane(mine, 0)
    first = swap(send, "dp", 1)
    act, slope = pl.pallas_call(
        act_kernel,
        out_shape=(struct((rows, hid)), struct((rows, hid), F32)),
        in_specs=[VMEM] * 2,
        out_specs=(VMEM,) * 2,
        name="act",
        **limits(4, 1),
    )(there, pre)
    acts = {0: act} | {k: swap(act, "dp", k) for k in range(1, n_dp) if k & (k - 1) == 0}
    out_weight, one, first, _ = lax.optimization_barrier((out_weight, one, first, act))
    two = round_plane(stacked(functools.partial(stack_kernel, (0, 0)), (mine, one), 2 * block, "pair"), 1)
    second = stacked(functools.partial(stack_kernel, (0, block)), (pass_on, first), 2 * block, "pass_on")
    second = swap(second, "dp", 2)
    held = pl.pallas_call(
        hold_kernel,
        out_shape=struct(out_weight.shape),
        in_specs=[HBM],
        out_specs=VMEM,
        scratch_shapes=[pltpu.SemaphoreType.DMA],
        name="hold",
        **limits(8),
    )(pinned(out_weight))

    second, held = lax.optimization_barrier((second, held))
    split = stacked(spread_kernel, (keep, first, second), n_dp * block, "parts")
    near_part = [split] + [swap(split, "ctx", k) for k in range(1, n_ctx)]
    far_part = [swap(x, "mp", 1) for x in near_part]

    grad = pl.pallas_call(
        grad_kernel,
        out_shape=struct((rows, hid)),
        in_specs=[VMEM] * 6,
        out_specs=VMEM,
        scratch_shapes=[pltpu.VMEM((rows, feat), BF16)],
        name="grad",
        **limits(8),
    )(mine, one, two, held, slope, back)
    relay, _ = lax.optimization_barrier(([acts[k] for k in sorted(acts)], grad))
    relay = dict(zip(sorted(acts), relay))
    for k in range(n_dp):
        if k not in acts:
            acts[k] = swap(relay[k ^ (k & -k)] if k ^ (k & -k) in relay else acts[k ^ (k & -k)], "dp", k & -k)
    returned = lax.all_to_all(grad.reshape(images, vit, hid), ("ctx", "mp"), 0, 0, tiled=True)

    right, total, bias_grad = pl.pallas_call(
        functools.partial(early_kernel, n_dp, n_ctx),
        out_shape=(struct((n_dp * rows, cols)), struct((hid, cols), F32), struct((1, cols), F32)),
        in_specs=[VMEM] * (2 * n_ctx + 1),
        out_specs=(VMEM,) * 3,
        name="early",
        **limits(12),
    )(*near_part, *far_part, act)
    wide = cols
    weight_grad = pl.pallas_call(
        late_kernel,
        out_shape=struct((hid, cols), F32),
        grid=(cols // wide,),
        in_specs=[VMEM] * (n_dp + 1),
        out_specs=pl.BlockSpec((hid, wide), lambda i: (0, i)),
        name="late",
        **limits(12),
    )(*(acts[k] for k in range(1, n_dp)), right, total)
    returned, weight_grad = lax.optimization_barrier((returned, weight_grad))
    returned = jnp.swapaxes(returned, 0, 1).reshape(vit, hidden)
    return (returned, weight_grad, bias_grad.reshape(-1))


def solution(mesh):
    n_dp, n_ctx, n_mp = (mesh.shape[a] for a in ("dp", "ctx", "mp"))
    placed = (
        P(("dp", "ctx"), None),
        P(("dp", "ctx", "mp"), None),
        P(("ctx", "mp"), None),
        P("dp", None, None),
        P("dp", None),
        P("dp", None, None),
    )

    def per_device(*args):
        hid, feat = args[2].shape
        rows = args[1].shape[0] * n_ctx * n_mp
        gather = (n_dp - 1) * rows * (hid + feat // n_dp) * 2
        scatter = hid * feat * 4 * (n_dp - 1) // n_dp
        fits = (n_dp, n_ctx, n_mp) == (4, 4, 2)
        return (gathered if fits and gather < scatter else reduced)(*args)

    return jax.shard_map(
        per_device,
        mesh=mesh,
        in_specs=placed,
        out_specs=(P(("dp", "ctx", "mp"), None), P(("ctx", "mp"), "dp"), P("dp")),
        check_vma=False,
    )
```

```python
import functools

import jax
import jax.numpy as jnp
from jax import lax
from jax.experimental import pallas as pl
from jax.experimental.pallas import tpu as pltpu
from jax.sharding import PartitionSpec as P

BF16 = jnp.bfloat16
F32 = jnp.float32
VMEM = pl.BlockSpec(memory_space=pltpu.VMEM)
ANY = pl.BlockSpec(memory_space=pl.ANY)
HBM = pl.BlockSpec(memory_space=pltpu.HBM)


def gelu_parts(x):
    cdf = 0.5 * (1.0 + lax.erf(x * 0.7071067811865476))
    pdf = jnp.exp(-0.5 * x * x) * 0.3989422804014327
    return (x * cdf, cdf + x * pdf)


def stream_rows(counts, order, length):
    total = counts.shape[0]
    vit_end = jnp.cumsum(counts)
    vit_start = vit_end - counts
    onehot = (order[:, None] == jnp.arange(total, dtype=jnp.int32)[None, :]).astype(jnp.int32)
    ordered = jnp.sum(onehot * counts[None, :], axis=1)
    place_start = jnp.cumsum(ordered) - ordered
    llm_start = jnp.sum(onehot * place_start[:, None], axis=0)
    shift = llm_start - vit_start
    rows = jnp.arange(length, dtype=jnp.int32)
    member = (rows[:, None] >= vit_start[None, :]) & (rows[:, None] < vit_end[None, :])
    return rows + jnp.sum(jnp.where(member, shift[None, :], 0), axis=1)


def reduced(llm_grad, merger_pre, out_weight, patch_counts, image_order, vision_rows):
    group_rows = merger_pre.shape[0] * lax.axis_size(("ctx", "mp"))
    stream = stream_rows(patch_counts.reshape(-1), image_order.reshape(-1), group_rows)
    own_places = vision_rows[0][lax.axis_index("ctx")]
    own_rows = llm_grad[own_places]
    stream_grad = lax.all_gather(own_rows, "ctx", axis=0, tiled=True)
    pre_cols = lax.all_to_all(merger_pre, ("ctx", "mp"), split_axis=1, concat_axis=0, tiled=True)
    row_grad = stream_grad[stream]
    value, slope = gelu_parts(pre_cols.astype(F32))
    act = value.astype(BF16)
    act_grad = lax.dot_general(row_grad, out_weight, (((1,), (1,)), ((), ())), preferred_element_type=F32)
    pre_grad = (act_grad * slope).astype(BF16)
    returned = lax.all_to_all(pre_grad, ("ctx", "mp"), split_axis=0, concat_axis=1, tiled=True)
    term = lax.dot_general(act, row_grad, (((0,), (0,)), ((), ())), preferred_element_type=F32)
    ones_row = jnp.ones((row_grad.shape[0],), BF16)
    bias_term = jnp.dot(ones_row, row_grad, preferred_element_type=F32)
    return (
        returned,
        lax.psum_scatter(term, "dp", scatter_dimension=1, tiled=True),
        lax.psum_scatter(bias_term, "dp", scatter_dimension=0, tiled=True),
    )


def cut_kernel(pre, blocks, sems):
    wide = blocks.shape[2]
    copies = [
        pltpu.make_async_copy(pre.at[:, i * wide : (i + 1) * wide], blocks.at[i], sems.at[i])
        for i in range(blocks.shape[0])
    ]
    for copy in copies:
        copy.start()
    for copy in copies:
        copy.wait()


def order_maps(ctx, n_ctx, counts, order, there, back):
    images, rows = order.shape[1], there.shape[0]
    block = rows // n_ctx
    up = lax.broadcasted_iota(jnp.int32, (images, images), 0)
    along = lax.broadcasted_iota(jnp.int32, (images, images), 1)
    order_row = order[...]

    def total(mask, values, axis):
        return jnp.sum(jnp.where(mask, values, 0).astype(F32), axis=axis, keepdims=True).astype(jnp.int32)

    same = up == along
    per = counts.shape[1]
    shard = lax.broadcasted_iota(jnp.int32, (images, counts.shape[2]), 1)
    image = lax.broadcasted_iota(jnp.int32, (images, counts.shape[2]), 0)
    count_col = jnp.zeros((images, 1), jnp.int32)
    for i in range(per):
        count_col += total(image == shard * per + i, counts[0, i : i + 1, :], 1)
    count_row = total(same, count_col, 0)
    order_col = total(same, order_row, 1)
    vit_start_row = total(up < along, count_col, 0)
    vit_start_col = total(along < up, count_row, 1)
    placed_row = total(order_row == up, count_col, 0)
    placed_col = total(order_col == along, count_row, 1)
    place_start_col = total(along < up, placed_row, 1)
    place_start_row = total(up < along, placed_col, 0)
    llm_start_row = total(order_col == along, place_start_col, 0)
    llm_start_col = total(order_row == up, place_start_row, 1)

    def received(shape, dim):
        at = lax.broadcasted_iota(jnp.int32, shape, dim)
        out = jnp.zeros(shape, jnp.int32)
        for k in range(n_ctx):
            inside = (at >= k * block) & (at < (k + 1) * block)
            out = jnp.where(inside, at + ((ctx ^ k) - k) * block, out)
        return out

    image = lax.broadcasted_iota(jnp.int32, (rows, images), 0)
    member = (image >= vit_start_row) & (image < vit_start_row + count_row)
    stream_col = lax.broadcasted_iota(jnp.int32, (rows, 1), 0) + total(member, llm_start_row - vit_start_row, 1)
    back[...] = (stream_col == received((1, rows), 1)).astype(F32).astype(BF16)
    image = lax.broadcasted_iota(jnp.int32, (images, rows), 1)
    member = (image >= vit_start_col) & (image < vit_start_col + count_col)
    stream_row = lax.broadcasted_iota(jnp.int32, (1, rows), 1) + total(member, llm_start_col - vit_start_col, 0)
    there[...] = (stream_row == received((rows, 1), 0)).astype(F32).astype(BF16)


def pick_kernel(n_ctx, *refs):
    inputs, (chosen, there, back), parts = refs[:4], refs[4:7], refs[7:10]
    local, sems = refs[10:14], refs[14]
    llm, places, counts, order = local
    group, ctx, core = (lax.axis_index(a) for a in ("dp", "ctx", "mp"))
    copies = [pltpu.make_async_copy(a, b, sems.at[i]) for i, (a, b) in enumerate(zip(inputs, local))]
    for copy in copies:
        copy.start()
    for copy in copies[1:]:
        copy.wait()
    order_maps(ctx, n_ctx, counts, order, there, back)
    own = places[0, pl.ds(ctx, 1), :]
    hot = (lax.broadcasted_iota(jnp.int32, (llm.shape[0], own.shape[1]), 0) == own).astype(BF16)
    copies[0].wait()
    chosen[...] = lax.dot_general(hot, llm[...], (((0,), (0,)), ((), ())), preferred_element_type=F32).astype(BF16)
    wide = parts[0].shape[1]
    for out, distances in zip(parts, ((0,), (2,), (1, 3))):
        for i, far in enumerate(distances):
            at = pl.ds(pl.multiple_of((2 * (group ^ far) + core) * wide, wide), wide)
            out[i * chosen.shape[0] : (i + 1) * chosen.shape[0]] = chosen[:, at]


def act_kernel(there, pre, act, slope):
    x = jnp.dot(there[...], pre[...], preferred_element_type=F32)
    value, grade = gelu_parts(x)
    act[...] = value.astype(BF16)
    slope[...] = grade


def stack_kernel(starts, *refs):
    parts, out = refs[:-1], refs[-1]
    at = 0
    for part, start in zip(parts, starts):
        rows = part.shape[0] - start
        out[at : at + rows] = part[start:]
        at += rows


def spread_kernel(keep, first, second, out):
    rows = keep.shape[0]
    out[:rows] = keep[...]
    out[rows : 2 * rows] = first[:rows]
    out[2 * rows :] = second[...]


def hold_kernel(source, out, sem):
    copy = pltpu.make_async_copy(source, out, sem)
    copy.start()
    copy.wait()


def grad_kernel(mine, one, side, two, weight, slope, back, out, rows):
    core = lax.axis_index("mp")
    block = mine.shape[0]
    for spot, piece in zip((0, 1 + core, 2 - core, 3), (mine, one, side, two)):
        rows[pl.ds(pl.multiple_of(spot * block, block), block)] = piece[...]
    grad = lax.dot_general(rows[...], weight[...], (((1,), (1,)), ((), ())), preferred_element_type=F32)
    grad = (grad * slope[...]).astype(BF16)
    out[...] = jnp.dot(back[...], grad, preferred_element_type=F32).astype(BF16)


def early_kernel(n_dp, n_ctx, *refs):
    near, far, (act, right, total, bias) = refs[:n_ctx], refs[n_ctx : 2 * n_ctx], refs[2 * n_ctx :]
    core = lax.axis_index("mp")
    rows, half = near[0].shape
    block = rows // n_dp
    for side, pieces in ((core, near), (1 - core, far)):
        columns = pl.ds(pl.multiple_of(side * half, half), half)
        for k, piece in enumerate(pieces):
            for i in range(n_dp):
                to = (i * n_ctx + k) * block
                right[to : to + block, columns] = piece[i * block : (i + 1) * block]
    ones = jnp.ones((8, right.shape[0]), BF16)
    bias[...] = jnp.dot(ones, right[...], preferred_element_type=F32)[:1]
    total[...] = lax.dot_general(
        act[...], right[: act.shape[0]], (((0,), (0,)), ((), ())), preferred_element_type=F32
    )


def late_kernel(*refs):
    acts, (right, total, out) = refs[:-3], refs[-3:]
    wide, rows = out.shape[1], acts[0].shape[0]
    at = pl.ds(pl.multiple_of(pl.program_id(0) * wide, wide), wide)
    sums = total[:, at]
    for i, act in enumerate(acts):
        piece = right[(i + 1) * rows : (i + 2) * rows, at]
        sums += lax.dot_general(act[...], piece, (((0,), (0,)), ((), ())), preferred_element_type=F32)
    out[...] = sums


def struct(shape, dtype=BF16):
    return jax.ShapeDtypeStruct(shape, dtype)


def limits(mebibytes, cost=1):
    return dict(
        compiler_params=pltpu.CompilerParams(vmem_limit_bytes=mebibytes << 20),
        cost_estimate=pl.CostEstimate(flops=cost, bytes_accessed=cost, transcendentals=0),
    )


def swap(x, axis, k):
    n = lax.axis_size(axis)
    return lax.ppermute(x, axis, [(i, i ^ k) for i in range(n)])


def pinned(x):
    return pltpu.with_memory_space_constraint(x, pltpu.HBM)


def round_plane(x, step):
    pairs = [(2 * c + m, 2 * (c ^ (1 << (m ^ step))) + m) for c in range(4) for m in range(2)]
    return lax.ppermute(x, ("ctx", "mp"), pairs)


def stacked(kernel, parts, rows, name):
    return pl.pallas_call(
        kernel,
        out_shape=struct((rows, parts[0].shape[1])),
        in_specs=[VMEM] * len(parts),
        out_specs=VMEM,
        name=name,
        **limits(4),
    )(*parts)


def gathered(llm_grad, merger_pre, out_weight, patch_counts, image_order, vision_rows):
    n_dp, n_ctx, n_mp = lax.axis_size("dp"), lax.axis_size("ctx"), lax.axis_size("mp")
    images = n_ctx * n_mp
    vit, hidden = merger_pre.shape
    hid, feat = out_weight.shape
    block = vision_rows.shape[-1]
    rows = n_ctx * block
    cols = feat // n_dp

    blocks = pl.pallas_call(
        cut_kernel,
        out_shape=struct((images, vit, hid)),
        in_specs=[ANY],
        out_specs=ANY,
        scratch_shapes=[pltpu.SemaphoreType.DMA((images,))],
        name="cut",
        **limits(4),
    )(merger_pre)
    llm_grad, blocks = lax.optimization_barrier((llm_grad, blocks))
    pre = lax.all_to_all(blocks, ("ctx", "mp"), 0, 0, tiled=True).reshape(rows, hid)

    inputs = (llm_grad, vision_rows, jnp.swapaxes(patch_counts, 1, 2), image_order)
    mine, there, back, keep, pass_on, send = pl.pallas_call(
        functools.partial(pick_kernel, n_ctx),
        out_shape=(struct((block, feat)),)
        + (struct((rows, rows)),) * 2
        + (struct((block, cols // 2)),) * 2
        + (struct((2 * block, cols // 2)),),
        in_specs=[HBM] * 4,
        out_specs=(VMEM,) * 6,
        scratch_shapes=[pltpu.VMEM(x.shape, x.dtype) for x in inputs]
        + [pltpu.SemaphoreType.DMA((4,))],
        name="pick",
        **limits(8),
    )(*(pinned(x) for x in inputs))

    one = round_plane(mine, 0)
    first = swap(send, "dp", 1)
    act, slope = pl.pallas_call(
        act_kernel,
        out_shape=(struct((rows, hid)), struct((rows, hid), F32)),
        in_specs=[VMEM] * 2,
        out_specs=(VMEM,) * 2,
        name="act",
        **limits(4, 1),
    )(there, pre)
    acts = {0: act} | {k: swap(act, "dp", k) for k in range(1, n_dp) if k & (k - 1) == 0}
    out_weight, one, first, _ = lax.optimization_barrier((out_weight, one, first, act))
    two, side = round_plane(one, 1), swap(one, "mp", 1)
    second = stacked(functools.partial(stack_kernel, (0, block)), (pass_on, first), 2 * block, "pass_on")
    second = swap(second, "dp", 2)
    held = pl.pallas_call(
        hold_kernel,
        out_shape=struct(out_weight.shape),
        in_specs=[HBM],
        out_specs=VMEM,
        scratch_shapes=[pltpu.SemaphoreType.DMA],
        name="hold",
        **limits(8),
    )(pinned(out_weight))

    second, held = lax.optimization_barrier((second, held))
    split = stacked(spread_kernel, (keep, first, second), n_dp * block, "parts")
    near_part = [split] + [swap(split, "ctx", k) for k in range(1, n_ctx)]
    far_part = [swap(x, "mp", 1) for x in near_part]

    grad = pl.pallas_call(
        grad_kernel,
        out_shape=struct((rows, hid)),
        in_specs=[VMEM] * 7,
        out_specs=VMEM,
        scratch_shapes=[pltpu.VMEM((rows, feat), BF16)],
        name="grad",
        **limits(8),
    )(mine, one, side, two, held, slope, back)
    relay, _ = lax.optimization_barrier(([acts[k] for k in sorted(acts)], grad))
    relay = dict(zip(sorted(acts), relay))
    for k in range(n_dp):
        if k not in acts:
            acts[k] = swap(relay[k ^ (k & -k)] if k ^ (k & -k) in relay else acts[k ^ (k & -k)], "dp", k & -k)
    returned = lax.all_to_all(grad.reshape(images, vit, hid), ("ctx", "mp"), 0, 0, tiled=True)

    right, total, bias_grad = pl.pallas_call(
        functools.partial(early_kernel, n_dp, n_ctx),
        out_shape=(struct((n_dp * rows, cols)), struct((hid, cols), F32), struct((1, cols), F32)),
        in_specs=[VMEM] * (2 * n_ctx + 1),
        out_specs=(VMEM,) * 3,
        name="early",
        **limits(12),
    )(*near_part, *far_part, act)
    wide = cols // 2
    weight_grad = pl.pallas_call(
        late_kernel,
        out_shape=struct((hid, cols), F32),
        grid=(cols // wide,),
        in_specs=[VMEM] * (n_dp + 1),
        out_specs=pl.BlockSpec((hid, wide), lambda i: (0, i)),
        name="late",
        **limits(12),
    )(*(acts[k] for k in range(1, n_dp)), right, total)
    returned, weight_grad = lax.optimization_barrier((returned, weight_grad))
    returned = jnp.swapaxes(returned, 0, 1).reshape(vit, hidden)
    return (returned, weight_grad, bias_grad.reshape(-1))


def solution(mesh):
    n_dp, n_ctx, n_mp = (mesh.shape[a] for a in ("dp", "ctx", "mp"))
    placed = (
        P(("dp", "ctx"), None),
        P(("dp", "ctx", "mp"), None),
        P(("ctx", "mp"), None),
        P("dp", None, None),
        P("dp", None),
        P("dp", None, None),
    )

    def per_device(*args):
        hid, feat = args[2].shape
        rows = args[1].shape[0] * n_ctx * n_mp
        gather = (n_dp - 1) * rows * (hid + feat // n_dp) * 2
        scatter = hid * feat * 4 * (n_dp - 1) // n_dp
        fits = (n_dp, n_ctx, n_mp) == (4, 4, 2)
        return (gathered if fits and gather < scatter else reduced)(*args)

    return jax.shard_map(
        per_device,
        mesh=mesh,
        in_specs=placed,
        out_specs=(P(("dp", "ctx", "mp"), None), P(("ctx", "mp"), "dp"), P("dp")),
        check_vma=False,
    )
```
